256 devices in a mesh: dp: 8 (over y, z_hi), seq: 4 (over x), tensor: 8 (over z_lo, core).
Axes of the slice: x: 4, y: 4, z: 8 (z_hi: 2, z_lo: 4; z = z_hi * 4 + z_lo), core: 2. Of those that a mesh axis runs over, the one named last changes fastest.
Arguments:
- rows: bfloat16 [8, 512, 4096], P('dp', 'seq', 'tensor'), may hold values from -6 to 6
- keys: bfloat16 [8, 1024, 4096], P('dp', 'seq', 'tensor'), may hold values from -6 to 6
- values: bfloat16 [8, 1024, 4096], P('dp', 'seq', 'tensor'), may hold values from -18 to 18
- target_ids: int32 [8, 512], P('dp', 'seq'), may hold values from 0 to 3, as said below
- source_ids: int32 [8, 1024], P('dp'), may hold values from 0 to 3, as said below
- row_counts: int32 [8, 4], P('dp'), may hold values from 32 to 128, as said below
- w_query: bfloat16 [4096, 4096], P(None, 'tensor'), may hold values from -0.09375 to 0.09375
- w_output: bfloat16 [4096, 4096], P('tensor'), may hold values from -0.09375 to 0.09375
- query_gain: float32 [4096], P('tensor'), may hold values from 0.3 to 2.5
- key_gain: float32 [4096], P('tensor'), may hold values from 0.3 to 2.5
- cotangent: bfloat16 [8, 512, 4096], P('dp', 'seq', 'tensor'), may hold values from -6 to 6
Outputs:
- branch: bfloat16 [8, 512, 4096], P('dp', 'seq', 'tensor')
- rows_grad: bfloat16 [8, 512, 4096], P('dp', 'seq', 'tensor')
- keys_grad: bfloat16 [8, 1024, 4096], P('dp', 'seq', 'tensor')
- values_grad: bfloat16 [8, 1024, 4096], P('dp', 'seq', 'tensor')
- query_weight_grad: float32 [4096, 4096], P(('dp', 'seq'), 'tensor')
- output_weight_grad: float32 [4096, 4096], P('tensor', ('dp', 'seq'))
The draws below stay inside these ranges and needn't reach their ends.
Inputs may be any that keep to these rules, and one draw needn't show every extreme that they name: `target_ids`: within a batch the ids never fall; every id from 0 to 3 labels one or more target slots. `source_ids`: within a batch the ids never fall; every id from 0 to 3 labels one or more encoder tokens. `row_counts`: in every batch some block is full.
All inputs are finite; a program needn't handle non-finite values.
Results may differ from the reference program's by a relative error of at most 0.03.
The reference program's roundings to bfloat16 on the way count: a program that leaves them out, or rounds other values in their place, can miss the bound.
Values may be sent and summed in bfloat16 or wider, within the bound.
No kernel may reach another device: no remote copies, remote signals or barrier semaphores. Data moves between devices by JAX's collectives and lax.ppermute only.
A program may use at most 128 MiB of HBM per device.

```python
import jax
import jax.numpy as jnp
from jax import lax

D = 4096
H = 64
HS = 64
TT_DEV = 128
NEX = 4
TGT = 512
ENC = 1024
BATCH = 8
N_SEQ = 4
N_TENSOR = 8


def cut_ids(key, length, count):
    cuts = jax.random.permutation(key, length - 1)[:count - 1] + 1
    places = jnp.arange(length, dtype=jnp.int32)
    return jnp.sum((cuts[None, :] <= places[:, None]).astype(jnp.int32), axis=1).astype(jnp.int32)


def draw_target_ids(key, part):
    key = jax.random.fold_in(key, 11)
    batch_keys = jax.random.split(key, BATCH)
    return jax.vmap(lambda single: cut_ids(single, TGT, NEX))(batch_keys)


def draw_source_ids(key, part):
    key = jax.random.fold_in(key, 17)
    batch_keys = jax.random.split(key, BATCH)
    return jax.vmap(lambda single: cut_ids(single, ENC, NEX))(batch_keys)


def draw_row_counts(key, part):
    key = jax.random.fold_in(key, 31)
    first, second = jax.random.split(key)
    counts = jax.random.randint(first, (BATCH, N_SEQ), TT_DEV // 4, TT_DEV + 1).astype(jnp.int32)
    full = jax.random.randint(second, (BATCH, 1), 0, N_SEQ).astype(jnp.int32)
    blocks = jnp.arange(N_SEQ, dtype=jnp.int32)[None, :]
    return jnp.where(blocks == full, TT_DEV, counts).astype(jnp.int32)


def draw_query_gain(key, part):
    key = jax.random.fold_in(key, 23)
    unit = jax.random.uniform(key, (H * HS,), jnp.float32)
    return 0.3 + 0.4 * unit


def draw_key_gain(key, part):
    key = jax.random.fold_in(key, 29)
    unit = jax.random.uniform(key, (H * HS,), jnp.float32)
    return 0.3 + 0.4 * unit


def block_scale(stream_key, dims, shards, least, largest):
    level, own = 1.0, jax.random.fold_in(stream_key, 6)
    for position, parts in shards:
        heights = jnp.exp(jax.random.uniform(jax.random.fold_in(own, position), (parts,), jnp.float32, least / len(shards), largest / len(shards)))
        level = level * jnp.repeat(heights, dims[position] // parts).reshape([-1 if axis == position else 1 for axis in range(len(dims))])
    return level


def normal_values(stream_key, dims, deviation, limit, shards=(), held_as=jnp.bfloat16):
    array = deviation * jax.random.normal(stream_key, dims, jnp.float32)
    if shards:
        array = array * block_scale(stream_key, dims, shards, -0.22, 0.18)
    return jnp.clip(array, -limit, limit).astype(held_as)


def setup_inputs(seed: int = 0) -> dict:
    streams_of = jax.random.split(jax.random.key(seed), 12)
    return {
        "rows": normal_values(streams_of[0], (BATCH, TGT, D), 1.0, 6.0, ((0, 8), (1, 4), (2, 8))),
        "keys": normal_values(streams_of[1], (BATCH, ENC, H * HS), 1.0, 6.0, ((0, 8), (1, 4), (2, 8))),
        "values": normal_values(streams_of[2], (BATCH, ENC, H * HS), 3.0, 18.0, ((0, 8), (1, 4), (2, 8))),
        "target_ids": draw_target_ids(jax.random.fold_in(streams_of[11], 71), 0),
        "source_ids": draw_source_ids(jax.random.fold_in(streams_of[11], 71), 0),
        "row_counts": draw_row_counts(jax.random.fold_in(streams_of[11], 71), 0),
        "w_query": normal_values(streams_of[6], (D, H * HS), D ** -0.5, 0.09375, ((1, 8),)),
        "w_output": normal_values(streams_of[7], (H * HS, D), (H * HS) ** -0.5, 0.09375, ((0, 8),)),
        "query_gain": draw_query_gain(jax.random.fold_in(streams_of[11], 71), 0),
        "key_gain": draw_key_gain(jax.random.fold_in(streams_of[11], 71), 0),
        "cotangent": normal_values(streams_of[10], (BATCH, TGT, D), 1.0, 6.0, ((0, 8), (1, 4), (2, 8))),
    }


EPS = 1e-06

def norm_fwd(tensor, gain):
    average = lax.optimization_barrier(jnp.mean(tensor, axis=-1, keepdims=True))
    centred = tensor - average
    variance = lax.optimization_barrier(jnp.mean(centred * centred, axis=-1, keepdims=True))
    inverse = lax.rsqrt(variance + EPS)
    normed = centred * inverse
    return (normed, inverse, normed * gain)

def norm_bwd(upstream, normed, inverse, gain):
    scaled = upstream * gain
    return inverse * (scaled - lax.optimization_barrier(jnp.mean(scaled, axis=-1, keepdims=True)) - normed * lax.optimization_barrier(jnp.mean(scaled * normed, axis=-1, keepdims=True)))

def rounded_sum(partials):
    low = lax.optimization_barrier(partials.astype(jnp.bfloat16))
    return lax.optimization_barrier(jnp.sum(low.astype(jnp.float32), axis=0))

def head_work(inputs, allowed, livef):
    q_head, k_head, v_head, g_head = inputs
    scores = jnp.dot(q_head, k_head.T)
    scores = jnp.where(allowed, scores, -jnp.inf)
    highest = lax.optimization_barrier(jnp.max(scores, axis=-1, keepdims=True))
    expo = jnp.exp(scores - highest)
    probs = expo / lax.optimization_barrier(jnp.sum(expo, axis=-1, keepdims=True)) * livef[:, None]
    plow = probs.astype(jnp.bfloat16).astype(jnp.float32)
    attended = jnp.dot(plow, v_head).astype(jnp.bfloat16)
    delta = lax.optimization_barrier(jnp.sum(g_head * attended.astype(jnp.float32), axis=-1))
    dprobs = jnp.dot(g_head, v_head.T)
    sgrad = (probs * (dprobs - delta[:, None])).astype(jnp.bfloat16).astype(jnp.float32)
    qn_grad = jnp.dot(sgrad, k_head)
    kn_parts = jnp.einsum('cts,ctd->csd', sgrad.reshape(N_SEQ, TT_DEV, ENC), q_head.reshape(N_SEQ, TT_DEV, HS))
    v_parts = jnp.einsum('cts,ctd->csd', plow.reshape(N_SEQ, TT_DEV, ENC), g_head.reshape(N_SEQ, TT_DEV, HS))
    return (attended, qn_grad, rounded_sum(kn_parts), rounded_sum(v_parts))

def one_batch(carry, inputs, w_query, w_output, query_gain, key_gain):
    states, keys_b, values_b, target_b, source_b, counts_b, cot_b = inputs
    width = H * HS
    group = width // N_TENSOR
    qgain = query_gain.reshape(H, HS)
    kgain = key_gain.reshape(H, HS)
    places = jnp.arange(TGT, dtype=jnp.int32)
    livef = (places % TT_DEV < counts_b[places // TT_DEV]).astype(jnp.float32)
    query = jnp.dot(states, w_query, preferred_element_type=jnp.float32)
    qhat, qinverse, qnormed = norm_fwd(query.reshape(TGT, H, HS), qgain)
    query_reduced_precision = qnormed.astype(jnp.bfloat16).astype(jnp.float32)
    khat, kinverse, normalized_keys = norm_fwd(keys_b.astype(jnp.float32).reshape(ENC, H, HS), kgain)
    key_reduced_precision = normalized_keys.astype(jnp.bfloat16).astype(jnp.float32)
    value_rows = values_b.astype(jnp.float32).reshape(ENC, H, HS)
    allowed = target_b[:, None] == source_b[None, :]
    att_grad = jnp.dot(cot_b, w_output.T, preferred_element_type=jnp.float32).astype(jnp.bfloat16)
    gradient_triple3 = att_grad.astype(jnp.float32).reshape(TGT, H, HS)

    def head_wise(head_inputs):
        return head_work(head_inputs, allowed, livef)
    head_attention, head_query_normed, head_key_normed, head_value_gradient = lax.map(head_wise, (jnp.transpose(query_reduced_precision, (1, 0, 2)), jnp.transpose(key_reduced_precision, (1, 0, 2)), jnp.transpose(value_rows, (1, 0, 2)), jnp.transpose(gradient_triple3, (1, 0, 2))))
    attended = jnp.transpose(head_attention, (1, 0, 2))
    qn_grad = jnp.transpose(head_query_normed, (1, 0, 2))
    kn_grad = jnp.transpose(head_key_normed, (1, 0, 2))
    flat = attended.reshape(TGT, width)
    out_parts = jnp.einsum('tgc,gcd->gtd', flat.reshape(TGT, N_TENSOR, group).astype(jnp.float32), w_output.reshape(N_TENSOR, group, D).astype(jnp.float32))
    branch = rounded_sum(out_parts).astype(jnp.bfloat16)
    query_grad = norm_bwd(qn_grad, qhat, qinverse, qgain).reshape(TGT, width).astype(jnp.bfloat16)
    keys_grad = norm_bwd(kn_grad, khat, kinverse, kgain).reshape(ENC, width).astype(jnp.bfloat16)
    values_grad = jnp.transpose(head_value_gradient, (1, 0, 2)).reshape(ENC, width).astype(jnp.bfloat16)
    x_parts = jnp.einsum('tgc,dgc->gtd', query_grad.reshape(TGT, N_TENSOR, group).astype(jnp.float32), w_query.reshape(D, N_TENSOR, group).astype(jnp.float32))
    rows_grad = rounded_sum(x_parts).astype(jnp.bfloat16)
    wq_acc = carry[0] + jnp.dot(states.T, query_grad, preferred_element_type=jnp.float32)
    wo_acc = carry[1] + jnp.dot(flat.T, cot_b, preferred_element_type=jnp.float32)
    return ((wq_acc, wo_acc), (branch, rows_grad, keys_grad, values_grad))

def reference(rows, keys, values, target_ids, source_ids, row_counts, w_query, w_output, query_gain, key_gain, cotangent):
    width = H * HS
    start = (jnp.zeros((D, width), jnp.float32), jnp.zeros((width, D), jnp.float32))

    def step(carry, inputs):
        return one_batch(carry, inputs, w_query, w_output, query_gain, key_gain)
    totals, stacked = lax.scan(step, start, (rows, keys, values, target_ids, source_ids, row_counts, cotangent))
    return (stacked[0], stacked[1], stacked[2], stacked[3], totals[0], totals[1])
```

```python
import jax
import jax.numpy as jnp
from jax import lax
from jax.experimental import pallas as pl
from jax.experimental.pallas import tpu as pltpu
from jax.sharding import PartitionSpec as P

HS = 64
EPS = 1e-06
BF = jnp.bfloat16
F32 = jnp.float32
LANES = 128
ID_ROWS = 16
VMEM = pl.BlockSpec(memory_space=pltpu.VMEM)
SMEM = pl.BlockSpec(memory_space=pltpu.SMEM)


def dot(a, b, ca, cb):
    return lax.dot_general(a, b, (((ca,), (cb,)), ((), ())), preferred_element_type=F32)


def block(index, size):
    return pl.ds(pl.multiple_of(index * size, size), size)


def call(kernel, outs, scratch=(), flops=0, moved=0, smem=1):
    def run(*args):
        return pl.pallas_call(
            kernel,
            out_shape=[jax.ShapeDtypeStruct(s, d) for s, d in outs],
            in_specs=[SMEM] * smem + [VMEM] * (len(args) - smem),
            out_specs=[VMEM] * len(outs),
            scratch_shapes=list(scratch),
            compiler_params=pltpu.CompilerParams(vmem_limit_bytes=48 * 1024 * 1024),
            cost_estimate=pl.CostEstimate(flops=flops, bytes_accessed=moved, transcendentals=0),
        )(*args)

    return run


def send(x, axis, offset):
    size = lax.axis_size(axis)
    return lax.ppermute(x, axis, [(i, i ^ offset) for i in range(size)])


def segment_mean(x):
    low = lax.broadcasted_iota(jnp.int32, x.shape, 1) < HS
    first = jnp.sum(jnp.where(low, x, 0.0), axis=-1, keepdims=True)
    second = jnp.sum(jnp.where(low, 0.0, x), axis=-1, keepdims=True)
    return jnp.where(low, first, second) * (1.0 / HS)


def norm_fwd(x):
    centred = x - segment_mean(x)
    inverse = lax.rsqrt(segment_mean(centred * centred) + EPS)
    return centred * inverse, inverse


def norm_bwd(upstream, normed, inverse, gain):
    scaled = upstream * gain
    return inverse * (scaled - segment_mean(scaled) - normed * segment_mean(scaled * normed))


def pack_kernel(place, keys, values, ids, *outs):
    s = place[0]
    own = keys.shape[0]
    row = jnp.broadcast_to(ids[...].astype(F32).astype(BF), (ID_ROWS, LANES))
    for k, out in enumerate(outs):
        at = block(s ^ k, LANES)
        out[:own, :LANES] = keys[:, at]
        out[:own, LANES:] = values[:, at]
        out[own:, :LANES] = row
        out[own:, LANES:] = row


def query_kernel(place, w, *refs):
    x, outs, acc = refs[:8], refs[8:12], refs[12]
    s, t = place[0], place[1]
    width = x[0].shape[1]
    total = None
    for j in range(8):
        part = dot(x[j][...], w[block(t ^ j, width), :], 1, 0)
        total = part if total is None else total + part
    acc[...] = total
    for k, out in enumerate(outs):
        out[...] = acc[:, block(s ^ k, LANES)]


def gradient_kernel(place, w, *refs):
    x, c, outs, tiles, acc = refs[:4], refs[4:12], refs[12:16], refs[16:20], refs[20]
    s, t = place[0], place[1]
    width = c[0].shape[1]
    total = None
    for j in range(8):
        part = dot(c[j][...], w[:, block(t ^ j, width)], 1, 1)
        total = part if total is None else total + part
    acc[...] = total.astype(BF)
    for k, out in enumerate(outs):
        out[...] = acc[:, block(s ^ k, LANES)]
    for k, tile in enumerate(tiles):
        at = block(s ^ k, LANES)
        for i in range(4):
            tile[i] = x[i][:, at]
            tile[4 + i] = c[2 * i][:, at]


def attention_kernel(place, counts, source, qgain, kgain, *refs):
    q_in, kv_in, g_in = refs[:4], refs[4:8], refs[8:12]
    att_out, dq_out, kv_out = refs[12], refs[13], refs[14:18]
    kn, vs, khat, kinv, qn, gs, pw, sg = refs[18:]
    s = place[0]
    own = kv_out[0].shape[0]
    rows = q_in[0].shape[0]
    qg = qgain[:, block(s, LANES)]
    kg = kgain[:, block(s, LANES)]
    for k in range(4):
        at = block(s ^ k, own)
        hat, inv = norm_fwd(kv_in[k][:own, :LANES].astype(F32))
        khat[at, :] = hat
        kinv[at, :] = inv
        kn[at, :] = (hat * kg).astype(BF)
        vs[at, :] = kv_in[k][:own, LANES:]
    low = lax.broadcasted_iota(jnp.int32, (rows, LANES), 1) < HS
    src = source[...].astype(F32)
    for k in range(4):
        blk = s ^ k
        at = block(blk, rows)
        ids = jnp.broadcast_to(kv_in[k][own:, :LANES].astype(F32)[:1], (rows, LANES))
        ids = jnp.transpose(ids)[:, :1]
        allowed = ids == src
        live = (lax.broadcasted_iota(jnp.int32, (rows, 1), 0) < counts[0, blk]).astype(F32)
        hat, inv = norm_fwd(q_in[k][...])
        query = (hat * qg).astype(BF)
        grad = g_in[k][...]
        qn[at, :] = query
        gs[at, :] = grad
        zero = jnp.zeros_like(query)
        attended, upstream = [], []
        for h in range(2):
            mine = low if h == 0 else jnp.logical_not(low)
            scores = dot(jnp.where(mine, query, zero), kn[...], 1, 1)
            scores = jnp.where(allowed, scores, -jnp.inf)
            expo = jnp.exp(scores - jnp.max(scores, axis=-1, keepdims=True))
            probs = expo * (live / jnp.sum(expo, axis=-1, keepdims=True))
            plow = probs.astype(BF)
            pw[h, at, :] = plow
            att = dot(plow, vs[...], 1, 0).astype(BF)
            attended.append(att)
            gh = jnp.where(mine, grad, zero)
            delta = jnp.sum(gh.astype(F32) * att.astype(F32), axis=-1, keepdims=True)
            dprobs = dot(gh, vs[...], 1, 1)
            sgrad = (probs * (dprobs - delta)).astype(BF)
            sg[h, at, :] = sgrad
            upstream.append(dot(sgrad, kn[...], 1, 0))
        att_out[at, :] = jnp.where(low, attended[0], attended[1])
        dq = norm_bwd(jnp.where(low, upstream[0], upstream[1]), hat, inv, qg)
        dq_out[at, :] = dq.astype(BF)
    wide = lax.broadcasted_iota(jnp.int32, (own, LANES), 1) < HS
    for k in range(4):
        at = block(s ^ k, own)
        dk = jnp.where(wide, dot(sg[0, :, at], qn[...], 0, 0), dot(sg[1, :, at], qn[...], 0, 0))
        dv = jnp.where(wide, dot(pw[0, :, at], gs[...], 0, 0), dot(pw[1, :, at], gs[...], 0, 0))
        kv_out[k][:, :LANES] = norm_bwd(dk, khat[at, :], kinv[at, :], kg).astype(BF)
        kv_out[k][:, LANES:] = dv.astype(BF)


def gather_tokens(place, parts, tile_refs, first, full, tiles):
    s, t, d = place[0], place[1], place[2]
    rows = tile_refs[0].shape[1]
    for k in range(4):
        full[:, block(s ^ k, LANES)] = parts[k][...]
    for k in range(4):
        at = block(s ^ k, rows)
        for i in range(4):
            for side in range(2):
                to = block((t ^ d) ^ (2 * i + side), LANES)
                tiles[at, to] = tile_refs[2 * k + side][first + i]


def output_kernel(place, w, *refs):
    parts, tile_refs = refs[:4], refs[4:12]
    keep, other, grads, full, tiles = refs[12], refs[13], refs[14:18], refs[18], refs[19]
    s, t = place[0], place[1]
    gather_tokens(place, parts, tile_refs, 4, full, tiles)
    rows = keep.shape[1]
    width = keep.shape[2]
    own = full[block(s, rows), :]
    for i in range(4):
        keep[i] = dot(own, w[:, block(t ^ (2 * i), width)], 1, 0).astype(BF)
        other[i] = dot(own, w[:, block(t ^ (2 * i + 1), width)], 1, 0).astype(BF)
    grad = dot(full[...], tiles[...], 0, 0).astype(BF)
    for m in range(4):
        for z in range(2):
            grads[m][z] = grad[:, (2 * m + z) * LANES : (2 * m + z + 1) * LANES]


def input_kernel(place, w, *refs):
    parts, tile_refs = refs[:4], refs[4:12]
    keep, other, grads, full, tiles = refs[12], refs[13], refs[14:18], refs[18], refs[19]
    s, t = place[0], place[1]
    gather_tokens(place, parts, tile_refs, 0, full, tiles)
    rows = keep.shape[1]
    width = keep.shape[2]
    own = full[block(s, rows), :]
    for i in range(4):
        keep[i] = dot(own, w[block(t ^ (2 * i), width), :], 1, 1).astype(BF)
        other[i] = dot(own, w[block(t ^ (2 * i + 1), width), :], 1, 1).astype(BF)
    grad = dot(tiles[...], full[...], 0, 0).astype(BF)
    for m in range(4):
        for z in range(2):
            grads[m][z] = grad[(2 * m + z) * LANES : (2 * m + z + 1) * LANES]


def unpack_kernel(place, *refs):
    parts, keys, values = refs[:4], refs[4], refs[5]
    s = place[0]
    for k in range(4):
        at = block(s ^ k, LANES)
        keys[:, at] = parts[k][:, :LANES]
        values[:, at] = parts[k][:, LANES:]


def pair_kernel(keep, got, *outs):
    for i, out in enumerate(outs):
        out[...] = (keep[i].astype(F32) + got[i].astype(F32)).astype(BF)


def gather_tensor(x):
    even = [x] + [send(x, "tensor", 2 * i) for i in range(1, 4)]
    odd = [send(e, "tensor", 1) for e in even]
    return [b for pair in zip(even, odd) for b in pair]


def scatter_tensor(keep, other):
    got = send(other, "tensor", 1)
    _, rows, width = keep.shape
    pairs = call(pair_kernel, [((rows, width), BF)] * 4, smem=0)(keep, got)
    total = pairs[0].astype(F32)
    for i in range(1, 4):
        total = total + send(pairs[i], "tensor", 2 * i).astype(F32)
    return total.astype(BF)


def scatter_dp(parts):
    total = parts[0].astype(F32)
    for m in range(1, 4):
        total = total + send(parts[m], "dp", 2 * m).astype(F32)
    return total[0] + send(total[1].astype(BF), "dp", 1).astype(F32)


def swap_seq(parts):
    return [parts[0]] + [send(parts[k], "seq", k) for k in range(1, 4)]


def body(
    rows,
    keys,
    values,
    target_ids,
    source_ids,
    row_counts,
    w_query,
    w_output,
    query_gain,
    key_gain,
    cotangent,
):
    tokens, width = rows.shape[1:]
    own = keys.shape[1]
    targets, sources = 4 * tokens, 4 * own
    place = jnp.stack([lax.axis_index("seq"), lax.axis_index("tensor"), lax.axis_index("dp")])
    place = place.astype(jnp.int32)
    big = 2 * tokens * width * 8 * width

    kv_sent = call(pack_kernel, [((own + ID_ROWS, 2 * LANES), BF)] * 4, moved=2**20)(
        place, keys[0], values[0], target_ids
    )
    states = gather_tensor(rows[0])
    kv = swap_seq(kv_sent)
    query = call(
        query_kernel,
        [((tokens, LANES), F32)] * 4,
        [pltpu.VMEM((tokens, width), F32)],
        flops=big,
        moved=5 * 2**20,
    )(place, w_query, *states)
    query = swap_seq(query)
    cots = gather_tensor(cotangent[0])
    out = call(
        gradient_kernel,
        [((tokens, LANES), BF)] * 4 + [((8, tokens, LANES), BF)] * 4,
        [pltpu.VMEM((tokens, width), BF)],
        flops=big,
        moved=5 * 2**20,
    )(place, w_output, *states[::2], *cots)
    grads = swap_seq(out[:4])
    tiles_even = swap_seq(out[4:])
    tiles = []
    for tile in tiles_even:
        tiles += [tile, send(tile, "tensor", 1)]

    out = call(
        attention_kernel,
        [((targets, LANES), BF)] * 2 + [((own, 2 * LANES), BF)] * 4,
        [
            pltpu.VMEM((sources, LANES), BF),
            pltpu.VMEM((sources, LANES), BF),
            pltpu.VMEM((sources, LANES), F32),
            pltpu.VMEM((sources, LANES), F32),
            pltpu.VMEM((targets, LANES), BF),
            pltpu.VMEM((targets, LANES), BF),
            pltpu.VMEM((2, targets, sources), BF),
            pltpu.VMEM((2, targets, sources), BF),
        ],
        flops=2 * 12 * targets * sources * LANES,
        moved=4 * 2**20,
        smem=2,
    )(
        place,
        row_counts,
        source_ids,
        query_gain.reshape(1, -1),
        key_gain.reshape(1, -1),
        *query,
        *kv,
        *grads,
    )
    attended, query_grad, kv_grads = out[0], out[1], out[2:]

    def share(x):
        return [x] + [send(x, "seq", k) for k in range(1, 4)]

    half = [((4, tokens, width), BF)] * 2
    scratch = [pltpu.VMEM((targets, width), BF), pltpu.VMEM((targets, 8 * LANES), BF)]
    out = call(
        output_kernel, half + [((2, width, LANES), BF)] * 4, scratch, flops=2 * big, moved=8 * 2**20
    )(place, w_output, *share(attended), *tiles)
    branch = scatter_tensor(out[0], out[1])
    output_weight_grad = scatter_dp(out[2:])
    out = call(
        input_kernel, half + [((2, LANES, width), BF)] * 4, scratch, flops=2 * big, moved=8 * 2**20
    )(place, w_query, *share(query_grad), *tiles)
    rows_grad = scatter_tensor(out[0], out[1])
    query_weight_grad = scatter_dp(out[2:])

    keys_grad, values_grad = call(unpack_kernel, [((own, width), BF)] * 2, moved=2**20)(
        place, *swap_seq(kv_grads)
    )
    return (
        branch[None],
        rows_grad[None],
        keys_grad[None],
        values_grad[None],
        query_weight_grad,
        output_weight_grad,
    )


def solution(mesh):
    in_specs = (
        P("dp", "seq", "tensor"),
        P("dp", "seq", "tensor"),
        P("dp", "seq", "tensor"),
        P("dp", "seq"),
        P("dp", None),
        P("dp", None),
        P(None, "tensor"),
        P("tensor", None),
        P("tensor"),
        P("tensor"),
        P("dp", "seq", "tensor"),
    )
    out_specs = (
        P("dp", "seq", "tensor"),
        P("dp", "seq", "tensor"),
        P("dp", "seq", "tensor"),
        P("dp", "seq", "tensor"),
        P(("dp", "seq"), "tensor"),
        P("tensor", ("dp", "seq")),
    )
    return jax.shard_map(body, mesh=mesh, in_specs=in_specs, out_specs=out_specs, check_vma=False)
```

```python
import jax
import jax.numpy as jnp
from jax import lax
from jax.experimental import pallas as pl
from jax.experimental.pallas import tpu as pltpu
from jax.sharding import PartitionSpec as P

HS = 64
EPS = 1e-06
BF = jnp.bfloat16
F32 = jnp.float32
LANES = 128
MIB = 1024 * 1024
VMEM = pl.BlockSpec(memory_space=pltpu.VMEM)
ANY = pl.BlockSpec(memory_space=pl.ANY)
SMEM = pl.BlockSpec(memory_space=pltpu.SMEM)


def dot(a, b, ca, cb):
    return lax.dot_general(a, b, (((ca,), (cb,)), ((), ())), preferred_element_type=F32)


def block(index, size):
    return pl.ds(pl.multiple_of(index * size, size), size)


def lane_block(p):
    return slice(p * LANES, (p + 1) * LANES)


def call(kernel, outs, scratch=(), smem=1, left=0, vmem=28 * MIB):
    def run(*args):
        return pl.pallas_call(
            kernel,
            out_shape=[jax.ShapeDtypeStruct(s, d) for s, d in outs],
            in_specs=[SMEM] * smem + [ANY] * left + [VMEM] * (len(args) - smem - left),
            out_specs=[VMEM] * len(outs),
            scratch_shapes=list(scratch),
            compiler_params=pltpu.CompilerParams(vmem_limit_bytes=vmem),
            cost_estimate=pl.CostEstimate(flops=1, bytes_accessed=1, transcendentals=0),
        )(*args)

    return run


def send(x, axis, offset):
    size = lax.axis_size(axis)
    return lax.ppermute(x, axis, [(i, i ^ offset) for i in range(size)])


def after(xs, deps):
    return lax.optimization_barrier((xs, deps))[0]


def segment_mean(x):
    low = lax.broadcasted_iota(jnp.int32, x.shape, 1) < HS
    first = jnp.sum(jnp.where(low, x, 0.0), axis=-1, keepdims=True)
    second = jnp.sum(jnp.where(low, 0.0, x), axis=-1, keepdims=True)
    return jnp.where(low, first, second) * (1.0 / HS)


def norm_fwd(x):
    centred = x - segment_mean(x)
    inverse = lax.rsqrt(segment_mean(centred * centred) + EPS)
    return centred * inverse, inverse


def norm_bwd(upstream, normed, inverse, gain):
    scaled = upstream * gain
    return inverse * (scaled - segment_mean(scaled) - normed * segment_mean(scaled * normed))


def prepare_kernel(keys, values, rows, cot, gain, both, out, khat, kinv, held, sems):
    width = keys.shape[1]
    copies = [
        pltpu.make_async_copy(keys, held, sems.at[0]),
        pltpu.make_async_copy(values, out.at[:, pl.ds(width, width)], sems.at[1]),
        pltpu.make_async_copy(rows, both.at[0], sems.at[2]),
        pltpu.make_async_copy(cot, both.at[1], sems.at[3]),
    ]
    for copy in copies:
        copy.start()
    copies[0].wait()
    for p in range(width // LANES):
        at = lane_block(p)
        hat, inv = norm_fwd(held[:, at].astype(F32))
        khat[:, at] = hat
        kinv[:, at] = inv
        out[:, at] = (hat * gain[:, at]).astype(BF)
    for copy in copies[1:]:
        copy.wait()


def query_kernel(place, w, *refs):
    x, out = refs[:8], refs[8]
    t = place[1]
    width = x[0].shape[2]
    total = None
    for j in range(8):
        part = dot(x[j][0], w[block(t ^ j, width), :], 1, 0)
        total = part if total is None else total + part
    out[...] = total


def gradient_kernel(place, w, *refs):
    x, out = refs[:8], refs[8]
    t = place[1]
    width = x[0].shape[2]
    total = None
    for j in range(8):
        part = dot(w[:, block(t ^ j, width)], x[j][1], 1, 1)
        total = part if total is None else total + part
    out[...] = jnp.transpose(total).astype(BF)


def cut_kernel(place, *refs):
    x, outs = refs[:4], refs[4:]
    s = place[0]
    for k, out in enumerate(outs):
        for i in range(4):
            for which in range(2):
                out[4 * which + i] = jnp.transpose(x[i][which, :, block(s ^ (k + 1), LANES)])


def forward_kernel(place, counts, source, target, qgain, query, *refs):
    kv, out, probs_out, keys, values, normed, qhat, qinv, ids = refs[:4], *refs[4:]
    s = place[0]
    rows, width = query.shape
    own = kv[0].shape[0]
    for k in range(4):
        keys[k * own : (k + 1) * own, :] = kv[k][:, :width]
        values[k * own : (k + 1) * own, :] = kv[k][:, width:]
        ids[:, k * own : (k + 1) * own] = source[:, block(s ^ k, own)]
    mine = jnp.transpose(jnp.broadcast_to(target[...].astype(F32), (rows, rows)))[:, :1]
    allowed = mine == ids[...].astype(F32)
    live = (lax.broadcasted_iota(jnp.int32, (rows, 1), 0) < counts[0, s]).astype(F32)
    low = lax.broadcasted_iota(jnp.int32, (rows, LANES), 1) < HS
    for p in range(width // LANES):
        at = lane_block(p)
        hat, inv = norm_fwd(query[:, at])
        qhat[:, at] = hat
        qinv[:, at] = inv
        q = (hat * qgain[:, at]).astype(BF)
        normed[:, at] = q
        zero = jnp.zeros_like(q)
        attended = []
        for h in range(2):
            head = low if h == 0 else jnp.logical_not(low)
            scores = dot(jnp.where(head, q, zero), keys[:, at], 1, 1)
            scores = jnp.where(allowed, scores, -jnp.inf)
            expo = jnp.exp(scores - jnp.max(scores, axis=-1, keepdims=True))
            probs = expo * (live / jnp.sum(expo, axis=-1, keepdims=True))
            probs_out[2 * p + h] = probs
            attended.append(dot(probs.astype(BF), values[:, at], 1, 0).astype(BF))
        out[:, at] = jnp.where(low, attended[0], attended[1])


def backward_kernel(qgain, grad, attended, probs, keys, values, qhat, qinv, out, sgrads):
    rows, width = grad.shape
    out[:, :width] = attended[...]
    low = lax.broadcasted_iota(jnp.int32, (rows, LANES), 1) < HS
    for p in range(width // LANES):
        at = lane_block(p)
        g = grad[:, at]
        zero = jnp.zeros_like(g)
        upstream = []
        for h in range(2):
            gh = jnp.where(low if h == 0 else jnp.logical_not(low), g, zero)
            delta = jnp.sum(gh.astype(F32) * attended[:, at].astype(F32), axis=-1, keepdims=True)
            sgrad = (probs[2 * p + h] * (dot(gh, values[:, at], 1, 1) - delta)).astype(BF)
            sgrads[2 * p + h] = sgrad
            upstream.append(dot(sgrad, keys[:, at], 1, 0))
        dq = jnp.where(low, upstream[0], upstream[1])
        out[:, lane_block(p + width // LANES)] = norm_bwd(dq, qhat[:, at], qinv[:, at], qgain[:, at]).astype(BF)


def partial_kernel(grad, normed, probs, sgrads, *outs):
    width = grad.shape[1]
    own = outs[0].shape[0]
    wide = lax.broadcasted_iota(jnp.int32, (4 * own, LANES), 1) < HS
    for p in range(width // LANES):
        at, other = lane_block(p), lane_block(p + width // LANES)
        dk = [dot(sgrads[2 * p + h], normed[:, at], 0, 0) for h in range(2)]
        dv = [dot(probs[2 * p + h].astype(BF), grad[:, at], 0, 0) for h in range(2)]
        dk = jnp.where(wide, dk[0], dk[1]).astype(BF)
        dv = jnp.where(wide, dv[0], dv[1]).astype(BF)
        for k, out in enumerate(outs):
            out[:, at] = dk[k * own : (k + 1) * own]
            out[:, other] = dv[k * own : (k + 1) * own]


def product_kernel(place, w_output, w_query, both, keep, other):
    t = place[1]
    width = w_query.shape[1]
    attended, query_grad = both[:, :width], both[:, width:]
    for j in range(8):
        out, i = (other if j % 2 else keep), j // 2
        out[0, i] = dot(attended, w_output[:, block(t ^ j, width)], 1, 0).astype(BF)
        part = dot(w_query[block(t ^ j, width), :], query_grad, 1, 1).astype(BF)
        out[1, i] = jnp.transpose(part)


def pair_kernel(keep, got, *outs):
    for i, out in enumerate(outs):
        out[...] = (keep[:, i].astype(F32) + got[:, i].astype(F32)).astype(BF)


def weight_kernel(place, *refs):
    x, parts, tiles, outs, full, across = refs[:8], refs[8:12], refs[12:18], refs[18:22], refs[22], refs[23]
    s, t, d = place[0], place[1], place[2]
    rows = parts[0].shape[0]
    width = x[0].shape[2]
    for k in range(4):
        full[k * rows : (k + 1) * rows, :] = parts[k][...]
    for which in range(2):
        for j in range(8):
            to = block((t ^ d) ^ j, LANES)
            across[which, to, :rows] = jnp.transpose(x[j][which, :, block(s, LANES)])
        for k in range(1, 4):
            at = slice(k * rows, (k + 1) * rows)
            for side in range(2):
                for i in range(4):
                    to = block((t ^ d) ^ (2 * i + side), LANES)
                    across[which, to, at] = tiles[2 * (k - 1) + side][4 * which + i]
    for m, out in enumerate(outs):
        for z in range(2):
            at = lane_block(2 * m + z)
            out[z, 0] = dot(across[0, at, :], full[:, width:], 1, 0).astype(BF)
            out[z, 1] = dot(across[1, at, :], full[:, :width], 1, 0).astype(BF)


def source_kernel(gain, khat, kinv, *refs):
    parts, keys, values = refs[:4], refs[4], refs[5]
    width = keys.shape[1]
    for p in range(width // LANES):
        at, other = lane_block(p), lane_block(p + width // LANES)
        dk = sum(part[:, at].astype(F32) for part in parts)
        dv = sum(part[:, other].astype(F32) for part in parts)
        keys[:, at] = norm_bwd(dk, khat[:, at], kinv[:, at], gain[:, at]).astype(BF)
        values[:, at] = dv.astype(BF)


def share(x):
    return [x] + [send(x, "seq", k) for k in range(1, 4)]


def total_of(parts):
    return sum(part.astype(F32) for part in parts)


def body(
    rows,
    keys,
    values,
    target_ids,
    source_ids,
    row_counts,
    w_query,
    w_output,
    query_gain,
    key_gain,
    cotangent,
):
    tokens, width = rows.shape[1:]
    own = keys.shape[1]
    place = jnp.stack([lax.axis_index("seq"), lax.axis_index("tensor"), lax.axis_index("dp")])
    place = place.astype(jnp.int32)
    qgain, kgain = query_gain.reshape(1, -1), key_gain.reshape(1, -1)
    line = (tokens, width)

    own_block, message, khat, kinv = call(
        prepare_kernel,
        [((2, tokens, width), BF), ((own, 2 * width), BF), ((own, width), F32), ((own, width), F32)],
        [pltpu.VMEM((own, width), BF), pltpu.SemaphoreType.DMA((4,))],
        smem=0,
        left=4,
        vmem=60 * MIB,
    )(keys[0], values[0], rows[0], cotangent[0], kgain)
    kv = share(message)
    even = [own_block] + [send(after(own_block, kv[3]) if i == 1 else own_block, "tensor", 2 * i) for i in range(1, 4)]
    even = [even[0], even[1], *after(even[2:], kv[1:3])]
    blocks = [b for e in even for b in (e, send(e, "tensor", 1))]
    query = call(query_kernel, [(line, F32)])(place, w_query, *blocks)[0]
    grad = call(gradient_kernel, [(line, BF)])(place, w_output, *blocks)[0]
    cut = call(cut_kernel, [((8, LANES, tokens), BF)] * 3)(place, *even)
    cut = [send(tile, "seq", k + 1) for k, tile in enumerate(cut)]
    tiles = [half for tile in cut for half in (tile, send(tile, "tensor", 1))]

    attended, probs, keys_all, values_all, normed, qhat, qinv = call(
        forward_kernel,
        [(line, BF), ((2 * width // LANES, tokens, 4 * own), F32), ((4 * own, width), BF), ((4 * own, width), BF)]
        + [(line, BF), (line, F32), (line, F32)],
        [pltpu.VMEM((1, 4 * own), jnp.int32)],
        smem=2,
    )(place, row_counts, source_ids, target_ids, qgain, query, *kv)
    both, sgrads = call(
        backward_kernel,
        [((tokens, 2 * width), BF), ((2 * width // LANES, tokens, 4 * own), BF)],
        smem=0,
    )(qgain, grad, attended, probs, keys_all, values_all, qhat, qinv)
    parts = share(both)
    kv_parts = call(partial_kernel, [((own, 2 * width), BF)] * 4, smem=0)(
        grad, normed, probs, after(sgrads, cut)
    )

    keep, other = call(product_kernel, [((2, 4, tokens, width), BF)] * 2)(
        place, w_output, w_query, after(both, cut)
    )
    got = send(after(other, parts[1]), "tensor", 1)
    pairs = call(pair_kernel, [((2, tokens, width), BF)] * 4, smem=0)(keep, got)
    lines = [pairs[0]] + [send(pairs[i], "tensor", 2 * i) for i in range(1, 4)]
    sums = call(
        weight_kernel,
        [((2, 2, LANES, width), BF)] * 4,
        [pltpu.VMEM((4 * tokens, 2 * width), BF), pltpu.VMEM((2, 8 * LANES, 4 * tokens), BF)],
    )(place, *blocks, *after(parts, (kv_parts, lines[1], lines[2])), *tiles)
    sums = total_of([sums[0]] + [send(sums[m], "dp", 2 * m) for m in range(1, 4)])
    lines = total_of(lines).astype(BF)
    kv_sums = [kv_parts[0]] + [send(after(kv_parts[k], lines), "seq", k) for k in (1, 3, 2)]
    weights = sums[0] + send(sums[1].astype(BF), "dp", 1).astype(F32)
    keys_grad, values_grad = call(source_kernel, [((own, width), BF)] * 2, smem=0)(
        kgain, khat, kinv, *kv_sums
    )
    return (
        lines[:1],
        lines[1:],
        keys_grad[None],
        values_grad[None],
        weights[0],
        weights[1].T,
    )


def solution(mesh):
    in_specs = (
        P("dp", "seq", "tensor"),
        P("dp", "seq", "tensor"),
        P("dp", "seq", "tensor"),
        P("dp", "seq"),
        P("dp", None),
        P("dp", None),
        P(None, "tensor"),
        P("tensor", None),
        P("tensor"),
        P("tensor"),
        P("dp", "seq", "tensor"),
    )
    out_specs = (
        P("dp", "seq", "tensor"),
        P("dp", "seq", "tensor"),
        P("dp", "seq", "tensor"),
        P("dp", "seq", "tensor"),
        P(("dp", "seq"), "tensor"),
        P("tensor", ("dp", "seq")),
    )
    return jax.shard_map(body, mesh=mesh, in_specs=in_specs, out_specs=out_specs, check_vma=False)
```

```python
import jax
import jax.numpy as jnp
from jax import lax
from jax.experimental import pallas as pl
from jax.experimental.pallas import tpu as pltpu
from jax.sharding import PartitionSpec as P

HS = 64
EPS = 1e-06
BF = jnp.bfloat16
F32 = jnp.float32
LANES = 128
MIB = 1024 * 1024
VMEM = pl.BlockSpec(memory_space=pltpu.VMEM)
ANY = pl.BlockSpec(memory_space=pl.ANY)
SMEM = pl.BlockSpec(memory_space=pltpu.SMEM)


def dot(a, b, ca, cb):
    return lax.dot_general(a, b, (((ca,), (cb,)), ((), ())), preferred_element_type=F32)


def block(index, size):
    return pl.ds(pl.multiple_of(index * size, size), size)


def lane_block(p):
    return slice(p * LANES, (p + 1) * LANES)


def call(kernel, outs, scratch=(), smem=1, left=0, vmem=28 * MIB):
    def run(*args):
        return pl.pallas_call(
            kernel,
            out_shape=[jax.ShapeDtypeStruct(s, d) for s, d in outs],
            in_specs=[SMEM] * smem + [ANY] * left + [VMEM] * (len(args) - smem - left),
            out_specs=[VMEM] * len(outs),
            scratch_shapes=list(scratch),
            compiler_params=pltpu.CompilerParams(vmem_limit_bytes=vmem),
            cost_estimate=pl.CostEstimate(flops=1, bytes_accessed=1, transcendentals=0),
        )(*args)

    return run


def send(x, axis, offset):
    size = lax.axis_size(axis)
    return lax.ppermute(x, axis, [(i, i ^ offset) for i in range(size)])


def after(xs, deps):
    return lax.optimization_barrier((xs, deps))[0]


def segment_mean(x):
    low = lax.broadcasted_iota(jnp.int32, x.shape, 1) < HS
    first = jnp.sum(jnp.where(low, x, 0.0), axis=-1, keepdims=True)
    second = jnp.sum(jnp.where(low, 0.0, x), axis=-1, keepdims=True)
    return jnp.where(low, first, second) * (1.0 / HS)


def norm_fwd(x):
    centred = x - segment_mean(x)
    inverse = lax.rsqrt(segment_mean(centred * centred) + EPS)
    return centred * inverse, inverse


def norm_bwd(upstream, normed, inverse, gain):
    scaled = upstream * gain
    return inverse * (scaled - segment_mean(scaled) - normed * segment_mean(scaled * normed))


def prepare_kernel(keys, values, rows, cot, gain, both, out, khat, kinv, held, sems):
    width = keys.shape[1]
    copies = [
        pltpu.make_async_copy(keys, held, sems.at[0]),
        pltpu.make_async_copy(values, out.at[:, pl.ds(width, width)], sems.at[1]),
        pltpu.make_async_copy(rows, both.at[0], sems.at[2]),
        pltpu.make_async_copy(cot, both.at[1], sems.at[3]),
    ]
    for copy in copies:
        copy.start()
    copies[0].wait()
    for p in range(width // LANES):
        at = lane_block(p)
        hat, inv = norm_fwd(held[:, at].astype(F32))
        khat[:, at] = hat
        kinv[:, at] = inv
        out[:, at] = (hat * gain[:, at]).astype(BF)
    for copy in copies[1:]:
        copy.wait()


def touch_kernel(w, out):
    out[...] = w[:16, :LANES]


def query_kernel(place, w, *refs):
    x, out = refs[:8], refs[9]
    t = place[1]
    width = x[0].shape[2]
    total = None
    for j in range(8):
        part = dot(x[j][0], w[block(t ^ j, width), :], 1, 0)
        total = part if total is None else total + part
    out[...] = total


def gradient_kernel(place, w, *refs):
    x, out = refs[:8], refs[8]
    t = place[1]
    width = x[0].shape[2]
    total = None
    for j in range(8):
        part = dot(w[:, block(t ^ j, width)], x[j][1], 1, 1)
        total = part if total is None else total + part
    out[...] = jnp.transpose(total).astype(BF)


def cut_kernel(place, *refs):
    x, outs = refs[:4], refs[4:]
    s = place[0]
    for k, out in enumerate(outs):
        for i in range(4):
            for which in range(2):
                out[4 * which + i] = jnp.transpose(x[i][which, :, block(s ^ (k + 1), LANES)])


def forward_kernel(place, counts, source, target, qgain, query, *refs):
    kv, out, probs_out, keys, values, normed, qhat, qinv, ids = refs[:4], *refs[4:]
    s = place[0]
    rows, width = query.shape
    own = kv[0].shape[0]
    for k in range(4):
        keys[k * own : (k + 1) * own, :] = kv[k][:, :width]
        values[k * own : (k + 1) * own, :] = kv[k][:, width:]
        ids[:, k * own : (k + 1) * own] = source[:, block(s ^ k, own)]
    mine = jnp.transpose(jnp.broadcast_to(target[...].astype(F32), (rows, rows)))[:, :1]
    allowed = mine == ids[...].astype(F32)
    live = (lax.broadcasted_iota(jnp.int32, (rows, 1), 0) < counts[0, s]).astype(F32)
    low = lax.broadcasted_iota(jnp.int32, (rows, LANES), 1) < HS
    for p in range(width // LANES):
        at = lane_block(p)
        hat, inv = norm_fwd(query[:, at])
        qhat[:, at] = hat
        qinv[:, at] = inv
        q = (hat * qgain[:, at]).astype(BF)
        normed[:, at] = q
        zero = jnp.zeros_like(q)
        attended = []
        for h in range(2):
            head = low if h == 0 else jnp.logical_not(low)
            scores = dot(jnp.where(head, q, zero), keys[:, at], 1, 1)
            scores = jnp.where(allowed, scores, -jnp.inf)
            expo = jnp.exp(scores - jnp.max(scores, axis=-1, keepdims=True))
            probs = expo * (live / jnp.sum(expo, axis=-1, keepdims=True))
            probs_out[2 * p + h] = probs
            attended.append(dot(probs.astype(BF), values[:, at], 1, 0).astype(BF))
        out[:, at] = jnp.where(low, attended[0], attended[1])


def backward_kernel(qgain, grad, attended, probs, keys, values, qhat, qinv, out, sgrads):
    rows, width = grad.shape
    out[:, :width] = attended[...]
    low = lax.broadcasted_iota(jnp.int32, (rows, LANES), 1) < HS
    for p in range(width // LANES):
        at = lane_block(p)
        g = grad[:, at]
        zero = jnp.zeros_like(g)
        upstream = []
        for h in range(2):
            gh = jnp.where(low if h == 0 else jnp.logical_not(low), g, zero)
            delta = jnp.sum(gh.astype(F32) * attended[:, at].astype(F32), axis=-1, keepdims=True)
            sgrad = (probs[2 * p + h] * (dot(gh, values[:, at], 1, 1) - delta)).astype(BF)
            sgrads[2 * p + h] = sgrad
            upstream.append(dot(sgrad, keys[:, at], 1, 0))
        dq = jnp.where(low, upstream[0], upstream[1])
        out[:, lane_block(p + width // LANES)] = norm_bwd(dq, qhat[:, at], qinv[:, at], qgain[:, at]).astype(BF)


def partial_kernel(grad, normed, probs, sgrads, *outs):
    width = grad.shape[1]
    own = outs[0].shape[0]
    wide = lax.broadcasted_iota(jnp.int32, (4 * own, LANES), 1) < HS
    for p in range(width // LANES):
        at, other = lane_block(p), lane_block(p + width // LANES)
        dk = [dot(sgrads[2 * p + h], normed[:, at], 0, 0) for h in range(2)]
        dv = [dot(probs[2 * p + h].astype(BF), grad[:, at], 0, 0) for h in range(2)]
        dk = jnp.where(wide, dk[0], dk[1]).astype(BF)
        dv = jnp.where(wide, dv[0], dv[1]).astype(BF)
        for k, out in enumerate(outs):
            out[:, at] = dk[k * own : (k + 1) * own]
            out[:, other] = dv[k * own : (k + 1) * own]


def product_kernel(place, w_output, w_query, both, keep, other):
    t = place[1]
    width = w_query.shape[1]
    attended, query_grad = both[:, :width], both[:, width:]
    for j in range(8):
        out, i = (other if j % 2 else keep), j // 2
        out[0, i] = dot(attended, w_output[:, block(t ^ j, width)], 1, 0).astype(BF)
        part = dot(w_query[block(t ^ j, width), :], query_grad, 1, 1).astype(BF)
        out[1, i] = jnp.transpose(part)


def pair_kernel(keep, got, *outs):
    for i, out in enumerate(outs):
        out[...] = (keep[:, i].astype(F32) + got[:, i].astype(F32)).astype(BF)


def weight_kernel(place, *refs):
    x, parts, tiles, outs, full, across = refs[:8], refs[8:12], refs[12:18], refs[18:22], refs[22], refs[23]
    s, t, d = place[0], place[1], place[2]
    rows = parts[0].shape[0]
    width = x[0].shape[2]
    for k in range(4):
        full[k * rows : (k + 1) * rows, :] = parts[k][...]
    for which in range(2):
        for j in range(8):
            to = block((t ^ d) ^ j, LANES)
            across[which, to, :rows] = jnp.transpose(x[j][which, :, block(s, LANES)])
        for k in range(1, 4):
            at = slice(k * rows, (k + 1) * rows)
            for side in range(2):
                for i in range(4):
                    to = block((t ^ d) ^ (2 * i + side), LANES)
                    across[which, to, at] = tiles[2 * (k - 1) + side][4 * which + i]
    for m, out in enumerate(outs):
        for z in range(2):
            at = lane_block(2 * m + z)
            out[z, 0] = dot(across[0, at, :], full[:, width:], 1, 0).astype(BF)
            out[z, 1] = dot(across[1, at, :], full[:, :width], 1, 0).astype(BF)


def source_kernel(gain, khat, kinv, *refs):
    parts, keys, values = refs[:4], refs[4], refs[5]
    width = keys.shape[1]
    for p in range(width // LANES):
        at, other = lane_block(p), lane_block(p + width // LANES)
        dk = sum(part[:, at].astype(F32) for part in parts)
        dv = sum(part[:, other].astype(F32) for part in parts)
        keys[:, at] = norm_bwd(dk, khat[:, at], kinv[:, at], gain[:, at]).astype(BF)
        values[:, at] = dv.astype(BF)


def last_kernel(near, far, query_out, output_out):
    query_out[...] = near[0] + far[0].astype(F32)
    output_out[...] = jnp.transpose(near[1] + far[1].astype(F32))


def share(x):
    return [x] + [send(x, "seq", k) for k in range(1, 4)]


def total_of(parts):
    return sum(part.astype(F32) for part in parts)


def body(
    rows,
    keys,
    values,
    target_ids,
    source_ids,
    row_counts,
    w_query,
    w_output,
    query_gain,
    key_gain,
    cotangent,
):
    tokens, width = rows.shape[1:]
    own = keys.shape[1]
    place = jnp.stack([lax.axis_index("seq"), lax.axis_index("tensor"), lax.axis_index("dp")])
    place = place.astype(jnp.int32)
    qgain, kgain = query_gain.reshape(1, -1), key_gain.reshape(1, -1)
    line = (tokens, width)

    own_block, message, khat, kinv = call(
        prepare_kernel,
        [((2, tokens, width), BF), ((own, 2 * width), BF), ((own, width), F32), ((own, width), F32)],
        [pltpu.VMEM((own, width), BF), pltpu.SemaphoreType.DMA((4,))],
        smem=0,
        left=4,
        vmem=60 * MIB,
    )(keys[0], values[0], rows[0], cotangent[0], kgain)
    even = [own_block] + [send(own_block, "tensor", 2 * i) for i in range(1, 4)]
    touched = call(touch_kernel, [((16, LANES), BF)], smem=0)(w_query)[0]
    kv = [message, send(message, "seq", 1), send(message, "seq", 3)]
    kv.insert(2, send(after(message, (kv[1:], touched)), "seq", 2))
    even = [even[0], even[1], *after(even[2:], (kv[1], kv[3]))]
    blocks = [b for e in even for b in (e, send(e, "tensor", 1))]
    query = call(query_kernel, [(line, F32)])(place, w_query, *blocks, touched)[0]
    grad = call(gradient_kernel, [(line, BF)])(place, w_output, *blocks)[0]
    cut = call(cut_kernel, [((8, LANES, tokens), BF)] * 3)(place, *even)
    cut = [send(tile, "seq", k + 1) for k, tile in enumerate(cut)]
    tiles = [half for tile in cut for half in (tile, send(tile, "tensor", 1))]

    attended, probs, keys_all, values_all, normed, qhat, qinv = call(
        forward_kernel,
        [(line, BF), ((2 * width // LANES, tokens, 4 * own), F32), ((4 * own, width), BF), ((4 * own, width), BF)]
        + [(line, BF), (line, F32), (line, F32)],
        [pltpu.VMEM((1, 4 * own), jnp.int32)],
        smem=2,
    )(place, row_counts, source_ids, target_ids, qgain, query, *kv)
    both, sgrads = call(
        backward_kernel,
        [((tokens, 2 * width), BF), ((2 * width // LANES, tokens, 4 * own), BF)],
        smem=0,
    )(qgain, grad, attended, probs, keys_all, values_all, qhat, qinv)
    parts = share(both)
    kv_parts = call(partial_kernel, [((own, 2 * width), BF)] * 4, smem=0)(
        grad, normed, probs, after(sgrads, cut)
    )

    keep, other = call(product_kernel, [((2, 4, tokens, width), BF)] * 2)(
        place, w_output, w_query, after(both, (cut, kv_parts))
    )
    got = send(after(other, parts), "tensor", 1)
    pairs = call(pair_kernel, [((2, tokens, width), BF)] * 4, smem=0)(keep, got)
    sums = call(
        weight_kernel,
        [((2, 2, LANES, width), BF)] * 4,
        [pltpu.VMEM((4 * tokens, 2 * width), BF), pltpu.VMEM((2, 8 * LANES, 4 * tokens), BF)],
    )(place, *blocks, *after(parts, (kv_parts, pairs)), *tiles)
    first = [send(sums[1], "dp", 2), send(sums[3], "dp", 6), send(after(kv_parts[1], sums), "seq", 1)]
    first += [send(after(kv_parts[3], sums), "seq", 3), send(pairs[2], "tensor", 4)]
    middle = after(sums[2], first[:4])
    pairs, kv_parts = after((pairs, kv_parts), first)
    lines = total_of([pairs[0], first[4], send(pairs[3], "tensor", 6), send(pairs[1], "tensor", 2)]).astype(BF)
    sums = total_of([sums[0], first[0], first[1], send(middle, "dp", 4)])
    kv_sums = [kv_parts[0], first[2], first[3], send(kv_parts[2], "seq", 2)]
    query_weight_grad, output_weight_grad = call(
        last_kernel, [((LANES, width), F32), ((width, LANES), F32)], smem=0
    )(sums[0], send(sums[1].astype(BF), "dp", 1))
    keys_grad, values_grad = call(source_kernel, [((own, width), BF)] * 2, smem=0)(
        kgain, khat, kinv, *kv_sums
    )
    return (
        lines[:1],
        lines[1:],
        keys_grad[None],
        values_grad[None],
        query_weight_grad,
        output_weight_grad,
    )


def solution(mesh):
    in_specs = (
        P("dp", "seq", "tensor"),
        P("dp", "seq", "tensor"),
        P("dp", "seq", "tensor"),
        P("dp", "seq"),
        P("dp", None),
        P("dp", None),
        P(None, "tensor"),
        P("tensor", None),
        P("tensor"),
        P("tensor"),
        P("dp", "seq", "tensor"),
    )
    out_specs = (
        P("dp", "seq", "tensor"),
        P("dp", "seq", "tensor"),
        P("dp", "seq", "tensor"),
        P("dp", "seq", "tensor"),
        P(("dp", "seq"), "tensor"),
        P("tensor", ("dp", "seq")),
    )
    return jax.shard_map(body, mesh=mesh, in_specs=in_specs, out_specs=out_specs, check_vma=False)
```

```python
import jax
import jax.numpy as jnp
from jax import lax
from jax.experimental import pallas as pl
from jax.experimental.pallas import tpu as pltpu
from jax.sharding import PartitionSpec as P

HS = 64
EPS = 1e-06
BF = jnp.bfloat16
F32 = jnp.float32
LANES = 128
MIB = 1024 * 1024
VMEM = pl.BlockSpec(memory_space=pltpu.VMEM)
ANY = pl.BlockSpec(memory_space=pl.ANY)
SMEM = pl.BlockSpec(memory_space=pltpu.SMEM)


def dot(a, b, ca, cb):
    return lax.dot_general(a, b, (((ca,), (cb,)), ((), ())), preferred_element_type=F32)


def block(index, size):
    return pl.ds(pl.multiple_of(index * size, size), size)


def lane_block(p):
    return slice(p * LANES, (p + 1) * LANES)


def call(kernel, outs, scratch=(), smem=1, left=0, vmem=28 * MIB):
    def run(*args):
        return pl.pallas_call(
            kernel,
            out_shape=[jax.ShapeDtypeStruct(s, d) for s, d in outs],
            in_specs=[SMEM] * smem + [ANY] * left + [VMEM] * (len(args) - smem - left),
            out_specs=[VMEM] * len(outs),
            scratch_shapes=list(scratch),
            compiler_params=pltpu.CompilerParams(vmem_limit_bytes=vmem),
            cost_estimate=pl.CostEstimate(flops=1, bytes_accessed=1, transcendentals=0),
        )(*args)

    return run


def send(x, axis, offset):
    size = lax.axis_size(axis)
    return lax.ppermute(x, axis, [(i, i ^ offset) for i in range(size)])


def after(xs, deps):
    return lax.optimization_barrier((xs, deps))[0]


def segment_mean(x):
    low = lax.broadcasted_iota(jnp.int32, x.shape, 1) < HS
    first = jnp.sum(jnp.where(low, x, 0.0), axis=-1, keepdims=True)
    second = jnp.sum(jnp.where(low, 0.0, x), axis=-1, keepdims=True)
    return jnp.where(low, first, second) * (1.0 / HS)


def norm_fwd(x):
    centred = x - segment_mean(x)
    inverse = lax.rsqrt(segment_mean(centred * centred) + EPS)
    return centred * inverse, inverse


def norm_bwd(upstream, normed, inverse, gain):
    scaled = upstream * gain
    return inverse * (scaled - segment_mean(scaled) - normed * segment_mean(scaled * normed))


def prepare_kernel(keys, values, rows, cot, gain, both, out, khat, kinv, held, sems):
    width = keys.shape[1]
    copies = [
        pltpu.make_async_copy(keys, held, sems.at[0]),
        pltpu.make_async_copy(values, out.at[:, pl.ds(width, width)], sems.at[1]),
        pltpu.make_async_copy(rows, both.at[0], sems.at[2]),
        pltpu.make_async_copy(cot, both.at[1], sems.at[3]),
    ]
    for copy in copies:
        copy.start()
    copies[0].wait()
    for p in range(width // LANES):
        at = lane_block(p)
        hat, inv = norm_fwd(held[:, at].astype(F32))
        khat[:, at] = hat
        kinv[:, at] = inv
        out[:, at] = (hat * gain[:, at]).astype(BF)
    for copy in copies[1:]:
        copy.wait()


def touch_kernel(w, out):
    out[...] = w[:16, :LANES]


def query_kernel(place, w, *refs):
    x, out = refs[:8], refs[9]
    t = place[1]
    width = x[0].shape[2]
    total = None
    for j in range(8):
        part = dot(x[j][0], w[block(t ^ j, width), :], 1, 0)
        total = part if total is None else total + part
    out[...] = total


def gradient_kernel(place, w, *refs):
    x, out = refs[:8], refs[8]
    t = place[1]
    width = x[0].shape[2]
    total = None
    for j in range(8):
        part = dot(w[:, block(t ^ j, width)], x[j][1], 1, 1)
        total = part if total is None else total + part
    out[...] = jnp.transpose(total).astype(BF)


def cut_kernel(place, *refs):
    x, outs = refs[:4], refs[4:]
    s = place[0]
    for k, out in enumerate(outs):
        for i in range(4):
            for which in range(2):
                out[4 * which + i] = jnp.transpose(x[i][which, :, block(s ^ (k + 1), LANES)])


def forward_kernel(place, counts, source, target, qgain, query, *refs):
    kv, out, probs_out, keys, values, normed, qhat, qinv, ids = refs[:4], *refs[4:]
    s = place[0]
    rows, width = query.shape
    own = kv[0].shape[0]
    for k in range(4):
        keys[k * own : (k + 1) * own, :] = kv[k][:, :width]
        values[k * own : (k + 1) * own, :] = kv[k][:, width:]
        ids[:, k * own : (k + 1) * own] = source[:, block(s ^ k, own)]
    mine = jnp.transpose(jnp.broadcast_to(target[...].astype(F32), (rows, rows)))[:, :1]
    allowed = mine == ids[...].astype(F32)
    live = (lax.broadcasted_iota(jnp.int32, (rows, 1), 0) < counts[0, s]).astype(F32)
    low = lax.broadcasted_iota(jnp.int32, (rows, LANES), 1) < HS
    for p in range(width // LANES):
        at = lane_block(p)
        hat, inv = norm_fwd(query[:, at])
        qhat[:, at] = hat
        qinv[:, at] = inv
        q = (hat * qgain[:, at]).astype(BF)
        normed[:, at] = q
        zero = jnp.zeros_like(q)
        attended = []
        for h in range(2):
            head = low if h == 0 else jnp.logical_not(low)
            scores = dot(jnp.where(head, q, zero), keys[:, at], 1, 1)
            scores = jnp.where(allowed, scores, -jnp.inf)
            expo = jnp.exp(scores - jnp.max(scores, axis=-1, keepdims=True))
            probs = expo * (live / jnp.sum(expo, axis=-1, keepdims=True))
            probs_out[2 * p + h] = probs
            attended.append(dot(probs.astype(BF), values[:, at], 1, 0).astype(BF))
        out[:, at] = jnp.where(low, attended[0], attended[1])


def backward_kernel(qgain, grad, attended, probs, keys, values, qhat, qinv, out, sgrads):
    rows, width = grad.shape
    out[:, :width] = attended[...]
    low = lax.broadcasted_iota(jnp.int32, (rows, LANES), 1) < HS
    for p in range(width // LANES):
        at = lane_block(p)
        g = grad[:, at]
        zero = jnp.zeros_like(g)
        upstream = []
        for h in range(2):
            gh = jnp.where(low if h == 0 else jnp.logical_not(low), g, zero)
            delta = jnp.sum(gh.astype(F32) * attended[:, at].astype(F32), axis=-1, keepdims=True)
            sgrad = (probs[2 * p + h] * (dot(gh, values[:, at], 1, 1) - delta)).astype(BF)
            sgrads[2 * p + h] = sgrad
            upstream.append(dot(sgrad, keys[:, at], 1, 0))
        dq = jnp.where(low, upstream[0], upstream[1])
        out[:, lane_block(p + width // LANES)] = norm_bwd(dq, qhat[:, at], qinv[:, at], qgain[:, at]).astype(BF)


def partial_kernel(grad, normed, probs, sgrads, *outs):
    width = grad.shape[1]
    own = outs[0].shape[0]
    wide = lax.broadcasted_iota(jnp.int32, (4 * own, LANES), 1) < HS
    for p in range(width // LANES):
        at, other = lane_block(p), lane_block(p + width // LANES)
        dk = [dot(sgrads[2 * p + h], normed[:, at], 0, 0) for h in range(2)]
        dv = [dot(probs[2 * p + h].astype(BF), grad[:, at], 0, 0) for h in range(2)]
        dk = jnp.where(wide, dk[0], dk[1]).astype(BF)
        dv = jnp.where(wide, dv[0], dv[1]).astype(BF)
        for k, out in enumerate(outs):
            out[:, at] = dk[k * own : (k + 1) * own]
            out[:, other] = dv[k * own : (k + 1) * own]


def product_kernel(place, w_output, w_query, both, keep, other):
    t = place[1]
    width = w_query.shape[1]
    attended, query_grad = both[:, :width], both[:, width:]
    for j in range(8):
        out, i = (other if j % 2 else keep), j // 2
        out[0, i] = dot(attended, w_output[:, block(t ^ j, width)], 1, 0).astype(BF)
        part = dot(w_query[block(t ^ j, width), :], query_grad, 1, 1).astype(BF)
        out[1, i] = jnp.transpose(part)


def pair_kernel(keep, got, *outs):
    for i, out in enumerate(outs):
        out[...] = (keep[:, i].astype(F32) + got[:, i].astype(F32)).astype(BF)


def weight_kernel(place, *refs):
    x, parts, tiles, outs, full, across = refs[:8], refs[8:12], refs[12:18], refs[18:22], refs[22], refs[23]
    s, t, d = place[0], place[1], place[2]
    rows = parts[0].shape[0]
    width = x[0].shape[2]
    for k in range(4):
        full[k * rows : (k + 1) * rows, :] = parts[k][...]
    for which in range(2):
        for j in range(8):
            to = block((t ^ d) ^ j, LANES)
            across[which, to, :rows] = jnp.transpose(x[j][which, :, block(s, LANES)])
        for k in range(1, 4):
            at = slice(k * rows, (k + 1) * rows)
            for side in range(2):
                for i in range(4):
                    to = block((t ^ d) ^ (2 * i + side), LANES)
                    across[which, to, at] = tiles[2 * (k - 1) + side][4 * which + i]
    for m, out in enumerate(outs):
        for z in range(2):
            at = lane_block(2 * m + z)
            out[z, 0] = dot(across[0, at, :], full[:, width:], 1, 0).astype(BF)
            out[z, 1] = dot(across[1, at, :], full[:, :width], 1, 0).astype(BF)


def source_kernel(gain, khat, kinv, *refs):
    parts, keys, values = refs[:4], refs[4], refs[5]
    width = keys.shape[1]
    for p in range(width // LANES):
        at, other = lane_block(p), lane_block(p + width // LANES)
        dk = sum(part[:, at].astype(F32) for part in parts)
        dv = sum(part[:, other].astype(F32) for part in parts)
        keys[:, at] = norm_bwd(dk, khat[:, at], kinv[:, at], gain[:, at]).astype(BF)
        values[:, at] = dv.astype(BF)


def last_kernel(near, far, query_out, output_out):
    query_out[...] = near[0] + far[0].astype(F32)
    output_out[...] = jnp.transpose(near[1] + far[1].astype(F32))


def share(x):
    return [x] + [send(x, "seq", k) for k in range(1, 4)]


def total_of(parts):
    return sum(part.astype(F32) for part in parts)


def body(
    rows,
    keys,
    values,
    target_ids,
    source_ids,
    row_counts,
    w_query,
    w_output,
    query_gain,
    key_gain,
    cotangent,
):
    tokens, width = rows.shape[1:]
    own = keys.shape[1]
    place = jnp.stack([lax.axis_index("seq"), lax.axis_index("tensor"), lax.axis_index("dp")])
    place = place.astype(jnp.int32)
    qgain, kgain = query_gain.reshape(1, -1), key_gain.reshape(1, -1)
    line = (tokens, width)

    own_block, message, khat, kinv = call(
        prepare_kernel,
        [((2, tokens, width), BF), ((own, 2 * width), BF), ((own, width), F32), ((own, width), F32)],
        [pltpu.VMEM((own, width), BF), pltpu.SemaphoreType.DMA((4,))],
        smem=0,
        left=4,
        vmem=60 * MIB,
    )(keys[0], values[0], rows[0], cotangent[0], kgain)
    even = [own_block] + [send(own_block, "tensor", 2 * i) for i in range(1, 4)]
    touched = call(touch_kernel, [((16, LANES), BF)], smem=0)(w_query)[0]
    kv = [message, send(message, "seq", 1), send(message, "seq", 3)]
    kv.insert(2, send(after(message, (kv[1:], touched)), "seq", 2))
    even = [even[0], even[1], *after(even[2:], (kv[1], kv[3]))]
    blocks = [b for e in even for b in (e, send(e, "tensor", 1))]
    query = call(query_kernel, [(line, F32)])(place, w_query, *blocks, touched)[0]
    grad = call(gradient_kernel, [(line, BF)])(place, w_output, *blocks)[0]
    cut = call(cut_kernel, [((8, LANES, tokens), BF)] * 3)(place, *even)
    cut = [send(tile, "seq", k + 1) for k, tile in enumerate(cut)]
    tiles = [half for tile in cut for half in (tile, send(tile, "tensor", 1))]

    attended, probs, keys_all, values_all, normed, qhat, qinv = call(
        forward_kernel,
        [(line, BF), ((2 * width // LANES, tokens, 4 * own), F32), ((4 * own, width), BF), ((4 * own, width), BF)]
        + [(line, BF), (line, F32), (line, F32)],
        [pltpu.VMEM((1, 4 * own), jnp.int32)],
        smem=2,
    )(place, row_counts, source_ids, target_ids, qgain, query, *kv)
    both, sgrads = call(
        backward_kernel,
        [((tokens, 2 * width), BF), ((2 * width // LANES, tokens, 4 * own), BF)],
        smem=0,
    )(qgain, grad, attended, probs, keys_all, values_all, qhat, qinv)
    parts = share(both)
    kv_parts = call(partial_kernel, [((own, 2 * width), BF)] * 4, smem=0)(
        grad, normed, probs, after(sgrads, cut)
    )

    keep, other = call(product_kernel, [((2, 4, tokens, width), BF)] * 2)(
        place, w_output, w_query, after(both, (cut, kv_parts))
    )
    got = send(after(other, parts), "tensor", 1)
    pairs = call(pair_kernel, [((2, tokens, width), BF)] * 4, smem=0)(keep, got)
    sums = call(
        weight_kernel,
        [((2, 2, LANES, width), BF)] * 4,
        [pltpu.VMEM((4 * tokens, 2 * width), BF), pltpu.VMEM((2, 8 * LANES, 4 * tokens), BF)],
    )(place, *blocks, *after(parts, (kv_parts, pairs)), *tiles)
    first = [send(sums[1], "dp", 2), send(sums[3], "dp", 6), send(pairs[2], "tensor", 4)]
    first += [send(pairs[1], "tensor", 2), send(after(kv_parts[1], sums), "seq", 1)]
    middle, third = after((sums[2], kv_parts[3]), first[:2])
    pairs, kv_parts = after((pairs, kv_parts), first)
    lines = total_of([pairs[0], first[2], first[3], send(pairs[3], "tensor", 6)]).astype(BF)
    sums = total_of([sums[0], first[0], first[1], send(middle, "dp", 4)])
    kv_sums = [kv_parts[0], first[4], send(third, "seq", 3), send(kv_parts[2], "seq", 2)]
    query_weight_grad, output_weight_grad = call(
        last_kernel, [((LANES, width), F32), ((width, LANES), F32)], smem=0
    )(sums[0], send(sums[1].astype(BF), "dp", 1))
    keys_grad, values_grad = call(source_kernel, [((own, width), BF)] * 2, smem=0)(
        kgain, khat, kinv, *kv_sums
    )
    return (
        lines[:1],
        lines[1:],
        keys_grad[None],
        values_grad[None],
        query_weight_grad,
        output_weight_grad,
    )


def solution(mesh):
    in_specs = (
        P("dp", "seq", "tensor"),
        P("dp", "seq", "tensor"),
        P("dp", "seq", "tensor"),
        P("dp", "seq"),
        P("dp", None),
        P("dp", None),
        P(None, "tensor"),
        P("tensor", None),
        P("tensor"),
        P("tensor"),
        P("dp", "seq", "tensor"),
    )
    out_specs = (
        P("dp", "seq", "tensor"),
        P("dp", "seq", "tensor"),
        P("dp", "seq", "tensor"),
        P("dp", "seq", "tensor"),
        P(("dp", "seq"), "tensor"),
        P("tensor", ("dp", "seq")),
    )
    return jax.shard_map(body, mesh=mesh, in_specs=in_specs, out_specs=out_specs, check_vma=False)
```
